32 devices in a mesh: wide: 8 (over z, core), lev: 4 (over y, x).
Axes of the slice: x: 2, y: 2, z: 4, core: 2. Of those that a mesh axis runs over, the one named last changes fastest.
Arguments:
- zonal_velocity_field: bfloat16 [4, 1280, 2688], P('lev', 'wide'), may hold values from -6 to 6
- meridional_velocity_field: bfloat16 [4, 1280, 2688], P('lev', 'wide'), may hold values from -6 to 6
- thermal_anomaly: bfloat16 [4, 1280, 2688], P('lev', 'wide'), may hold values from -6 to 6
- surface_orography: bfloat16 [1280, 2688], P('wide'), may hold values from -6 to 6
- layer_pressure_depth: float32 [4], replicated, may hold values from 0.2 to 1
- samples_each_circle: int32 [1280], P(('wide', 'lev')), may hold values from 12 to 2576, as said below
- position_zonal_orders: int32 [128], replicated, may hold values from 0 to 127, as said below
- scaled_associated_functions: bfloat16 [64, 640, 256], P(('wide', 'lev')), may hold values from -3 to 3
Outputs:
- spectra: bfloat16 [64, 2, 4, 2, 256], P(('wide', 'lev'))
The draws below stay inside these ranges and needn't reach their ends.
Inputs may be any that keep to these rules, and one draw needn't show every extreme that they name: `samples_each_circle`: row j has 16 + 4 * (min(j, 1279 - j) + e) points, e one of -1, 0, 1; e = 1 on the two rows next to the equator. `position_zonal_orders`: A permutation of the wavenumbers in which slots 2q and 2q + 1 hold two wavenumbers that add up to 127.
All inputs are finite; a program needn't handle non-finite values.
Results may differ from the reference program's by a relative error of at most 0.0065.
Values may be sent and summed in bfloat16 or wider, within the bound.
A program may use at most 64 MiB of HBM per device.

```python
import math
import jax
import jax.numpy as jnp
from jax import lax

PARALLEL_CIRCLES = 1280
MW = 128
NF = 2
NHALF = 640
CIRCLE_SAMPLES = 2688
VERTICAL_LAYERS = 4
NPAIR = 64
TABLE_COLS = 256


def draw_samples_each_circle(key, part):
    rows = jnp.arange(PARALLEL_CIRCLES, dtype=jnp.int32)
    polar = jnp.minimum(rows, PARALLEL_CIRCLES - 1 - rows)
    jitter = jax.random.randint(key, (PARALLEL_CIRCLES,), -1, 2).astype(jnp.int32)
    jitter = jnp.where(polar == NHALF - 1, 1, jitter)
    return (16 + 4 * (polar + jitter)).astype(jnp.int32)


def draw_position_zonal_orders(key, part):
    halves = MW // 2
    order = jax.random.permutation(jax.random.fold_in(key, 1), halves).astype(jnp.int32)
    flips = jax.random.randint(jax.random.fold_in(key, 2), (halves,), 0, 2).astype(jnp.int32)
    first_wave = jnp.where(flips == 1, MW - 1 - order, order)
    second_wave = MW - 1 - first_wave
    return jnp.stack([first_wave, second_wave], axis=1).reshape(MW).astype(jnp.int32)


def level_of(key, shape, pieces, least, largest):
    factor_of = 1.0
    for dim, blocks in pieces:
        draws = jax.random.uniform(jax.random.fold_in(jax.random.fold_in(key, 6), dim), (blocks,), jnp.float32, least / len(pieces), largest / len(pieces))
        factor_of = factor_of * jnp.repeat(jnp.exp(draws), shape[dim] // blocks).reshape((-1,) + (1,) * (len(shape) - 1 - dim))
    return factor_of


def normal_values(rng, shape, spread, bound, shards=(), held_as=jnp.bfloat16):
    level = level_of(rng, shape, shards, -0.22, 0.18) if shards else 1.0
    array = jax.random.normal(rng, shape, jnp.float32) * spread * level
    return jnp.minimum(jnp.maximum(array, -bound), bound).astype(held_as)


def setup_inputs(seed: int = 0) -> dict:
    key_of = jax.random.split(jax.random.key(seed), 9)
    return {
        "zonal_velocity_field": normal_values(key_of[0], (VERTICAL_LAYERS, PARALLEL_CIRCLES, CIRCLE_SAMPLES), 1.0, 6.0, ((0, 4), (1, 8))),
        "meridional_velocity_field": normal_values(key_of[1], (VERTICAL_LAYERS, PARALLEL_CIRCLES, CIRCLE_SAMPLES), 1.0, 6.0, ((0, 4), (1, 8))),
        "thermal_anomaly": normal_values(key_of[2], (VERTICAL_LAYERS, PARALLEL_CIRCLES, CIRCLE_SAMPLES), 1.0, 6.0, ((0, 4), (1, 8))),
        "surface_orography": normal_values(key_of[3], (PARALLEL_CIRCLES, CIRCLE_SAMPLES), 1.0, 6.0, ((0, 8),)),
        "layer_pressure_depth": jnp.clip(jnp.exp(jax.random.uniform(key_of[4], (VERTICAL_LAYERS,), jnp.float32, math.log(0.2), math.log(1.0))), 0.2, 1.0),
        "samples_each_circle": draw_samples_each_circle(jax.random.fold_in(key_of[8], 71), 0),
        "position_zonal_orders": draw_position_zonal_orders(jax.random.fold_in(key_of[8], 71), 0),
        "scaled_associated_functions": normal_values(key_of[7], (NPAIR, NHALF, TABLE_COLS), 0.5, 3.0, ((0, 32),)),
    }


circle = 2.0 * math.pi


def fourier_rows(fields, lengths, waves):
    rows_block = fields.shape[0]
    channels = fields.shape[1]
    sample_tally = fields.shape[2]
    blocks_high = sample_tally // 128
    count = waves.shape[0]
    position = jnp.arange(sample_tally, dtype=jnp.int32)
    masked = jnp.where(position[None, None, :] < lengths[:, None, None], fields.astype(jnp.float32), 0.0)
    masked = masked.reshape(rows_block, channels, blocks_high, 128)
    lengths_float = lengths.astype(jnp.float32)
    lower_index = jnp.arange(128, dtype=jnp.int32)
    inner_phase = (lower_index[None, :, None] * waves[None, None, :]) % lengths[:, None, None]
    inner_angle = inner_phase.astype(jnp.float32) * circle / lengths_float[:, None, None]
    inner_table = jnp.concatenate([jnp.cos(inner_angle), jnp.sin(inner_angle)], axis=2)
    partial_sums = jnp.einsum("rcha,ram->rchm", masked, inner_table, precision=lax.Precision.HIGHEST)
    part_cos = partial_sums[..., :count]
    part_sin = partial_sums[..., count:]
    upper_index = jnp.arange(blocks_high, dtype=jnp.int32) * 128
    outer_phase = (upper_index[None, :, None] * waves[None, None, :]) % lengths[:, None, None]
    outer_angle = outer_phase.astype(jnp.float32) * circle / lengths_float[:, None, None]
    outer_cos = jnp.cos(outer_angle)[:, None]
    outer_sin = jnp.sin(outer_angle)[:, None]
    real_part = jnp.sum(part_cos * outer_cos - part_sin * outer_sin, axis=2)
    imag_part = -jnp.sum(part_cos * outer_sin + part_sin * outer_cos, axis=2)
    keep = 2 * waves[None, :] < lengths[:, None]
    factor = jnp.where(keep, 1.0 / lengths_float[:, None], 0.0)[:, None, :]
    return jnp.stack([real_part * factor, imag_part * factor], axis=1)


def legendre_pair(data, table, first_wave, waves_total):
    half = table.shape[0]
    width = table.shape[1]
    north_rows = data[:half].astype(jnp.float32)
    south_rows = data[half:][::-1].astype(jnp.float32)
    even_part = (north_rows + south_rows).astype(jnp.bfloat16)
    odd_part = (north_rows - south_rows).astype(jnp.bfloat16)
    stacked = jnp.stack([even_part[..., 0], odd_part[..., 0], even_part[..., 1], odd_part[..., 1]], axis=1)
    stacked = stacked.reshape(half, -1)
    product = jnp.dot(stacked.T, table, preferred_element_type=jnp.float32).reshape(4, -1, width)
    column = jnp.arange(width, dtype=jnp.int32)
    split_at = waves_total - first_wave
    in_first = column < split_at
    in_second = jnp.logical_and(column >= split_at, column <= waves_total)
    chosen = jnp.where(in_first, column % 2, 2 + (column - split_at) % 2)
    picked = product[3]
    picked = jnp.where(chosen == 2, product[2], picked)
    picked = jnp.where(chosen == 1, product[1], picked)
    picked = jnp.where(chosen == 0, product[0], picked)
    result = jnp.where(jnp.logical_or(in_first, in_second), picked, 0.0)
    return result.reshape(2, data.shape[2], data.shape[3], width)


def reference(zonal_velocity_field, meridional_velocity_field, thermal_anomaly, surface_orography, layer_pressure_depth, samples_each_circle, position_zonal_orders, scaled_associated_functions):
    thermal_anomaly_single = thermal_anomaly.astype(jnp.float32)
    quadrature_scaled = thermal_anomaly_single * layer_pressure_depth[:, None, None]
    geopotential = surface_orography.astype(jnp.float32)[None] + jnp.cumsum(quadrature_scaled[::-1], axis=0)[::-1]
    east = zonal_velocity_field.astype(jnp.float32)
    northern_half = meridional_velocity_field.astype(jnp.float32)
    energy = (geopotential + 0.5 * (east * east + northern_half * northern_half)).astype(jnp.bfloat16)
    transport_product = (northern_half * thermal_anomaly_single).astype(jnp.bfloat16)
    fields = jnp.stack([energy, transport_product], axis=1).transpose(2, 0, 1, 3).reshape(PARALLEL_CIRCLES, VERTICAL_LAYERS * NF, CIRCLE_SAMPLES)
    block_rows = math.gcd(PARALLEL_CIRCLES, 16)
    shaped = fields.reshape(PARALLEL_CIRCLES // block_rows, block_rows, VERTICAL_LAYERS * NF, CIRCLE_SAMPLES)
    len_shaped = samples_each_circle.reshape(PARALLEL_CIRCLES // block_rows, block_rows)
    coefficients = lax.map(lambda item: fourier_rows(item[0], item[1], position_zonal_orders), (shaped, len_shaped))
    coefficients = coefficients.reshape(PARALLEL_CIRCLES, 2, VERTICAL_LAYERS, NF, MW).astype(jnp.bfloat16)
    paired = coefficients.reshape(PARALLEL_CIRCLES, 2, VERTICAL_LAYERS, NF, NPAIR, 2).transpose(4, 0, 1, 2, 3, 5)
    firsts = position_zonal_orders.reshape(NPAIR, 2)[:, 0]
    result = lax.map(lambda item: legendre_pair(item[0], item[1], item[2], MW), (paired, scaled_associated_functions, firsts))
    return result.astype(jnp.bfloat16)
```

```python
import functools

import jax
import jax.numpy as jnp
from jax import lax
from jax.experimental import pallas as pl
from jax.experimental.pallas import tpu as pltpu
from jax.sharding import PartitionSpec as P

STRIP = 16
LANES = 128
COS = (0.9999992251396179, -19.738981246948242, 64.92865753173828, -85.27162170410156, 58.79049301147461, -21.07110595703125)
SIN = (6.283185005187988, -41.341590881347656, 81.59994506835938, -76.61447143554688, 41.3428840637207, -12.471243858337402)


def horner(coefs, z):
    value = jnp.full_like(z, coefs[-1])
    for c in coefs[-2::-1]:
        value = value * z + c
    return value


def unit(n, length, inverse):
    turns = jnp.round(n * inverse)
    t = (n - turns * length) * inverse
    z = t * t
    return horner(COS, z), t * horner(SIN, z)


def times(a, b):
    return a[0] * b[0] - a[1] * b[1], a[0] * b[1] + a[1] * b[0]


def transform(high, high_pad, lens, scale, waves, lens_col, u, v, temp, oro, out, spread, sums, gathered):
    step = pl.program_id(0)
    steps = pl.num_programs(0)
    rows = steps * STRIP
    south = lax.axis_index("wide") * 2 >= lax.axis_size("wide")
    depth = scale[0]
    ground = scale[1]
    limit = jnp.broadcast_to(lens_col[...], (STRIP, LANES))
    lane = lax.broadcasted_iota(jnp.int32, (STRIP, LANES), 1)
    for h in range(high_pad):
        at = pl.ds(h * STRIP, STRIP)
        if h >= high:
            for c in range(3):
                spread[c, at, :] = jnp.zeros((STRIP, LANES), jnp.float32)
            continue
        cols = pl.ds(h * LANES, LANES)
        east = u[:, cols].astype(jnp.float32)
        north = v[:, cols].astype(jnp.float32)
        heat = temp[:, cols].astype(jnp.float32)
        weighted = heat * depth + oro[:, cols].astype(jnp.float32) * ground
        energy = 0.5 * (east * east + north * north) + weighted
        inside = lane + h * LANES < limit
        spread[0, at, :] = jnp.where(inside, energy, 0.0)
        spread[1, at, :] = jnp.where(inside, weighted, 0.0)
        spread[2, at, :] = jnp.where(inside, north * heat, 0.0)

    sub = lax.broadcasted_iota(jnp.int32, (8, LANES), 0).astype(jnp.float32)
    chunks = waves.shape[1] // LANES
    for chunk in range(chunks):
        m = jnp.broadcast_to(waves[:, chunk * LANES:(chunk + 1) * LANES], (8, LANES))

        def one_row(r, carry):
            length = lens[0, step * STRIP + r]
            inverse = lens[1, step * STRIP + r]
            data = jnp.concatenate(
                [spread[c, pl.ds(r, high_pad, stride=STRIP), :] for c in range(3)], axis=0
            ).astype(jnp.bfloat16)
            tiles = [unit(m * sub, length, inverse)]
            turn = unit(m * 8.0, length, inverse)
            while len(tiles) < LANES // 8:
                tiles = tiles + [times(tile, turn) for tile in tiles]
                turn = times(turn, turn)
            table = jnp.concatenate(
                [
                    jnp.concatenate([tile[0] for tile in tiles], axis=0),
                    jnp.concatenate([tile[1] for tile in tiles], axis=0),
                ],
                axis=1,
            ).astype(jnp.bfloat16)
            part = jnp.dot(data, table, preferred_element_type=jnp.float32)
            outer = [
                unit(m * (sub * float(LANES) + float(8 * LANES * g)), length, inverse)
                for g in range(high_pad // 8)
            ]
            place = jnp.where(south, STRIP - 1 - r, r)
            for c in range(3):
                real = jnp.zeros((8, LANES), jnp.float32)
                imag = jnp.zeros((8, LANES), jnp.float32)
                for g in range(high_pad // 8):
                    base = c * high_pad + g * 8
                    pc = part[base:base + 8, :LANES]
                    ps = part[base:base + 8, LANES:]
                    oc, os = outer[g]
                    real = real + (pc * oc - ps * os)
                    imag = imag - (pc * os + ps * oc)
                at = pl.ds(pl.multiple_of(place * 8, 8), 8)
                sums[2 * c, at, :] = real
                sums[2 * c + 1, at, :] = imag
            return carry

        lax.fori_loop(0, STRIP, one_row, 0, unroll=4)

        block = jnp.where(south, steps - 1 - step, step) * STRIP
        lens_here = jnp.broadcast_to(lens_col[...], (STRIP, LANES)).astype(jnp.float32)
        backward = lax.broadcasted_iota(jnp.int32, (STRIP, LANES), 0)
        m16 = jnp.broadcast_to(waves[:, chunk * LANES:(chunk + 1) * LANES], (STRIP, LANES))
        factor = jnp.zeros((STRIP, LANES), jnp.float32)
        for r in range(STRIP):
            length = lens[0, step * STRIP + r]
            inverse = lens[1, step * STRIP + r]
            place = jnp.where(south, STRIP - 1 - r, r)
            factor = jnp.where(
                backward == place, jnp.where(2.0 * m16 < length, inverse, 0.0), factor
            )
        for k in range(6):
            total = sums[k, pl.ds(0, STRIP, stride=8), :]
            for s in range(1, 8):
                total = total + sums[k, pl.ds(s, STRIP, stride=8), :]
            at = pl.ds(pl.multiple_of(k * rows + block, STRIP), STRIP)
            gathered[chunk, at, :] = total * factor

    @pl.when(step == 0)
    def _():
        tail = gathered.shape[1] - 6 * rows
        if tail:
            for chunk in range(chunks):
                gathered[chunk, 6 * rows:, :] = jnp.zeros((tail, LANES), jnp.float32)

    @pl.when(step == steps - 1)
    def _():
        for chunk in range(chunks):
            for b in range(gathered.shape[1] // LANES):
                out[chunk * LANES:(chunk + 1) * LANES, b * LANES:(b + 1) * LANES] = (
                    gathered[chunk, b * LANES:(b + 1) * LANES, :].T.astype(out.dtype)
                )


def local(u, v, temp, oro, depths, lens, orders, table):
    lev_count = lax.axis_size("lev")
    wide_count = lax.axis_size("wide")
    lev = lax.axis_index("lev")
    wide = lax.axis_index("wide")
    rows = temp.shape[1]
    samples = temp.shape[2]
    waves_total = orders.shape[0]
    high = samples // LANES
    high_pad = -(-high // 8) * 8
    steps = rows // STRIP
    packed = -(-6 * rows // LANES) * LANES
    band = lax.all_gather(lens, "lev", tiled=True)
    band_float = band.astype(jnp.float32)
    scale = jnp.stack(
        [lax.dynamic_index_in_dim(depths, lev, 0, False), (lev == lev_count - 1).astype(jnp.float32)]
    )
    smem = pl.BlockSpec(memory_space=pltpu.SMEM)
    field = pl.BlockSpec((STRIP, samples), lambda i: (i, 0))
    field3 = pl.BlockSpec((None, STRIP, samples), lambda i: (0, i, 0))
    coefs = pl.pallas_call(
        functools.partial(transform, high, high_pad),
        grid=(steps,),
        out_shape=jax.ShapeDtypeStruct((waves_total, packed), jnp.bfloat16),
        in_specs=[
            smem,
            smem,
            pl.BlockSpec((1, waves_total), lambda i: (0, 0)),
            pl.BlockSpec((STRIP, 1), lambda i: (i, 0)),
            field3,
            field3,
            field3,
            field,
        ],
        out_specs=pl.BlockSpec((waves_total, packed), lambda i: (0, 0)),
        scratch_shapes=[
            pltpu.VMEM((3, high_pad * STRIP, LANES), jnp.float32),
            pltpu.VMEM((6, STRIP * 8, LANES), jnp.float32),
            pltpu.VMEM((waves_total // LANES, packed, LANES), jnp.float32),
        ],
        compiler_params=pltpu.CompilerParams(vmem_limit_bytes=40 * 2**20),
    )(
        jnp.stack([band_float, 1.0 / band_float]),
        scale,
        orders.astype(jnp.float32)[None],
        band[:, None],
        u,
        v,
        temp,
        oro,
    )
    devices = lev_count * wide_count
    slots = waves_total // devices
    got = lax.all_to_all(
        coefs.reshape(devices, slots, packed), ("wide", "lev"), split_axis=0, concat_axis=0, tiled=True
    )
    got = got[:, :, :6 * rows].astype(jnp.float32)
    got = got.reshape(wide_count, lev_count, slots, 3, 2, rows)
    under = got[:, :, :, 1]
    below = jnp.cumsum(under[:, ::-1], axis=1)[:, ::-1] - under
    fields = jnp.stack([got[:, :, :, 0] + below, got[:, :, :, 2]], axis=3)
    half = wide_count // 2
    upper = fields[:half]
    lower = fields[half:][::-1]
    both = jnp.stack([upper + lower, upper - lower], axis=0).astype(jnp.bfloat16)
    both = both.transpose(3, 0, 5, 2, 4, 1, 6)
    pairs = slots // 2
    width = table.shape[2]
    both = both.reshape(pairs, -1, half * rows)
    product = jnp.einsum("pkj,pjc->pkc", both, table, preferred_element_type=jnp.float32)
    product = product.reshape(pairs, 4, 2, lev_count, 2, width)
    mine = lax.dynamic_slice_in_dim(orders, (wide * lev_count + lev) * slots, slots)
    first = mine.reshape(pairs, 2)[:, :1]
    column = jnp.arange(width, dtype=jnp.int32)[None]
    split = waves_total - first
    chosen = jnp.where(column < split, column % 2, 2 + (column - split) % 2)
    chosen = jnp.where(column <= waves_total, chosen, 4)[:, None, None, None, :]
    result = jnp.zeros_like(product[:, 0])
    for k in range(4):
        result = jnp.where(chosen == k, product[:, k], result)
    return result.astype(jnp.bfloat16)


def solution(mesh):
    in_specs = (
        P("lev", "wide", None),
        P("lev", "wide", None),
        P("lev", "wide", None),
        P("wide", None),
        P(),
        P(("wide", "lev")),
        P(),
        P(("wide", "lev"), None, None),
    )
    out_specs = P(("wide", "lev"), None, None, None, None)
    return jax.shard_map(local, mesh=mesh, in_specs=in_specs, out_specs=out_specs, check_vma=False)
```

```python
import functools

import jax
import jax.numpy as jnp
from jax import lax
from jax.experimental import pallas as pl
from jax.experimental.pallas import tpu as pltpu
from jax.sharding import PartitionSpec as P

STRIP = 16
LANES = 128
COS = (0.9999992251396179, -19.738981246948242, 64.92865753173828, -85.27162170410156, 58.79049301147461, -21.07110595703125)
SIN = (6.283185005187988, -41.341590881347656, 81.59994506835938, -76.61447143554688, 41.3428840637207, -12.471243858337402)


def horner(coefs, z):
    value = jnp.full_like(z, coefs[-1])
    for c in coefs[-2::-1]:
        value = value * z + c
    return value


def unit(n, length, inverse):
    turns = jnp.round(n * inverse)
    t = (n - turns * length) * inverse
    z = t * t
    return horner(COS, z), t * horner(SIN, z)


def times(a, b):
    return a[0] * b[0] - a[1] * b[1], a[0] * b[1] + a[1] * b[0]


MESH = pl.DeviceIdType.MESH


def swap(axes, x, out, landed, send_sem, recv_sem):
    sizes = [lax.axis_size(a) for a in axes]
    count = 1
    me = 0
    for a, size in zip(axes, sizes):
        count = count * size
        me = me * size + lax.axis_index(a)
    shared = x.shape[0] != count

    def device(turn):
        peer = lax.rem(me + turn, count)
        if len(axes) == 1:
            return peer, {axes[0]: peer}
        return peer, {axes[0]: lax.div(peer, sizes[1]), axes[1]: lax.rem(peer, sizes[1])}

    barrier = pltpu.get_barrier_semaphore()

    def greet(turn, carry):
        pl.semaphore_signal(barrier, inc=1, device_id=device(turn)[1], device_id_type=MESH)
        return carry

    lax.fori_loop(1, count, greet, 0)
    pl.semaphore_wait(barrier, count - 1)

    def copy(turn):
        peer, where = device(turn)
        return pltpu.make_async_remote_copy(
            src_ref=x.at[0 if shared else peer],
            dst_ref=landed.at[me],
            send_sem=send_sem.at[turn],
            recv_sem=recv_sem.at[turn],
            device_id=where,
            device_id_type=MESH,
        )

    def begin(turn, carry):
        copy(turn).start()
        return carry

    def finish(turn, carry):
        copy(turn).wait()
        return carry

    lax.fori_loop(1, count, begin, 0)
    landed[me] = x[0 if shared else me]
    lax.fori_loop(1, count, finish, 0)
    out[...] = landed[...]


def exchange(x, axes, count, number):
    shape = (count,) + x.shape[1:]
    vmem = pl.BlockSpec(memory_space=pltpu.VMEM)
    return pl.pallas_call(
        functools.partial(swap, axes),
        out_shape=jax.ShapeDtypeStruct(shape, x.dtype),
        in_specs=[vmem],
        out_specs=vmem,
        scratch_shapes=[
            pltpu.VMEM(shape, x.dtype),
            pltpu.SemaphoreType.DMA((count,)),
            pltpu.SemaphoreType.DMA((count,)),
        ],
        compiler_params=pltpu.CompilerParams(
            collective_id=number, has_side_effects=True, vmem_limit_bytes=24 * 2**20
        ),
    )(x)


def transform(high, high_pad, lens, depths, waves, u, v, temp, oro, out, spread, sums, gathered):
    step = pl.program_id(0)
    steps = pl.num_programs(0)
    rows = steps * STRIP
    south = lax.axis_index("wide") * 2 >= lax.axis_size("wide")
    level = lax.axis_index("lev")
    depth = depths[level]
    ground = jnp.where(level == lax.axis_size("lev") - 1, 1.0, 0.0)
    share = rows // lens.shape[0]

    def row_length(r):
        row = step * STRIP + r
        return lens[lax.div(row, share), 0, lax.rem(row, share)]

    backward = lax.broadcasted_iota(jnp.int32, (STRIP, LANES), 0)
    limit = jnp.zeros((STRIP, LANES), jnp.int32)
    for r in range(STRIP):
        limit = jnp.where(backward == r, row_length(r), limit)
    lane = lax.broadcasted_iota(jnp.int32, (STRIP, LANES), 1)
    for h in range(high_pad):
        at = pl.ds(h * STRIP, STRIP)
        if h >= high:
            for c in range(3):
                spread[c, at, :] = jnp.zeros((STRIP, LANES), jnp.float32)
            continue
        cols = pl.ds(h * LANES, LANES)
        east = u[:, cols].astype(jnp.float32)
        north = v[:, cols].astype(jnp.float32)
        heat = temp[:, cols].astype(jnp.float32)
        weighted = heat * depth + oro[:, cols].astype(jnp.float32) * ground
        energy = 0.5 * (east * east + north * north) + weighted
        inside = lane + h * LANES < limit
        spread[0, at, :] = jnp.where(inside, energy, 0.0)
        spread[1, at, :] = jnp.where(inside, weighted, 0.0)
        spread[2, at, :] = jnp.where(inside, north * heat, 0.0)

    sub = lax.broadcasted_iota(jnp.int32, (8, LANES), 0).astype(jnp.float32)
    chunks = waves.shape[1] // LANES
    for chunk in range(chunks):
        m = jnp.broadcast_to(waves[:, chunk * LANES:(chunk + 1) * LANES], (8, LANES))

        def one_row(r, carry):
            length = jnp.broadcast_to(row_length(r).astype(jnp.float32), (8, LANES))
            inverse = 1.0 / length
            data = jnp.concatenate(
                [spread[c, pl.ds(r, high_pad, stride=STRIP), :] for c in range(3)], axis=0
            ).astype(jnp.bfloat16)
            tiles = [unit(m * sub, length, inverse)]
            turn = unit(m * 8.0, length, inverse)
            while len(tiles) < LANES // 8:
                tiles = tiles + [times(tile, turn) for tile in tiles]
                turn = times(turn, turn)
            table = jnp.concatenate(
                [
                    jnp.concatenate([tile[0] for tile in tiles], axis=0),
                    jnp.concatenate([tile[1] for tile in tiles], axis=0),
                ],
                axis=1,
            ).astype(jnp.bfloat16)
            part = jnp.dot(data, table, preferred_element_type=jnp.float32)
            outer = [
                unit(m * (sub * float(LANES) + float(8 * LANES * g)), length, inverse)
                for g in range(high_pad // 8)
            ]
            place = jnp.where(south, STRIP - 1 - r, r)
            for c in range(3):
                real = jnp.zeros((8, LANES), jnp.float32)
                imag = jnp.zeros((8, LANES), jnp.float32)
                for g in range(high_pad // 8):
                    base = c * high_pad + g * 8
                    pc = part[base:base + 8, :LANES]
                    ps = part[base:base + 8, LANES:]
                    oc, os = outer[g]
                    real = real + (pc * oc - ps * os)
                    imag = imag - (pc * os + ps * oc)
                at = pl.ds(pl.multiple_of(place * 8, 8), 8)
                sums[2 * c, at, :] = real
                sums[2 * c + 1, at, :] = imag
            return carry

        lax.fori_loop(0, STRIP, one_row, 0, unroll=4)

        block = jnp.where(south, steps - 1 - step, step) * STRIP
        m16 = jnp.broadcast_to(waves[:, chunk * LANES:(chunk + 1) * LANES], (STRIP, LANES))
        length = jnp.zeros((STRIP, LANES), jnp.int32)
        for r in range(STRIP):
            place = jnp.where(south, STRIP - 1 - r, r)
            length = jnp.where(backward == place, row_length(r), length)
        length = length.astype(jnp.float32)
        factor = jnp.where(2.0 * m16 < length, 1.0 / length, 0.0)
        for k in range(6):
            total = sums[k, pl.ds(0, STRIP, stride=8), :]
            for s in range(1, 8):
                total = total + sums[k, pl.ds(s, STRIP, stride=8), :]
            at = pl.ds(pl.multiple_of(k * rows + block, STRIP), STRIP)
            gathered[chunk, at, :] = total * factor

    @pl.when(step == 0)
    def _():
        tail = gathered.shape[1] - 6 * rows
        if tail:
            for chunk in range(chunks):
                gathered[chunk, 6 * rows:, :] = jnp.zeros((tail, LANES), jnp.float32)

    @pl.when(step == steps - 1)
    def _():
        for chunk in range(chunks):
            for b in range(gathered.shape[1] // LANES):
                out[chunk * LANES:(chunk + 1) * LANES, b * LANES:(b + 1) * LANES] = (
                    gathered[chunk, b * LANES:(b + 1) * LANES, :].T.astype(out.dtype)
                )


def local(u, v, temp, oro, depths, lens, orders, table):
    lev_count = lax.axis_size("lev")
    wide_count = lax.axis_size("wide")
    lev = lax.axis_index("lev")
    wide = lax.axis_index("wide")
    rows = temp.shape[1]
    samples = temp.shape[2]
    waves_total = orders.shape[0]
    high = samples // LANES
    high_pad = -(-high // 8) * 8
    steps = rows // STRIP
    packed = -(-6 * rows // LANES) * LANES
    wide_held = -(-lens.shape[0] // LANES) * LANES
    held = jnp.pad(lens, (0, wide_held - lens.shape[0])).reshape(1, 1, wide_held)
    band = exchange(held, ("lev",), lev_count, 1)
    smem = pl.BlockSpec(memory_space=pltpu.SMEM)
    field = pl.BlockSpec((STRIP, samples), lambda i: (i, 0))
    field3 = pl.BlockSpec((None, STRIP, samples), lambda i: (0, i, 0))
    coefs = pl.pallas_call(
        functools.partial(transform, high, high_pad),
        grid=(steps,),
        out_shape=jax.ShapeDtypeStruct((waves_total, packed), jnp.bfloat16),
        in_specs=[
            smem,
            smem,
            pl.BlockSpec((1, waves_total), lambda i: (0, 0)),
            field3,
            field3,
            field3,
            field,
        ],
        out_specs=pl.BlockSpec((waves_total, packed), lambda i: (0, 0)),
        scratch_shapes=[
            pltpu.VMEM((3, high_pad * STRIP, LANES), jnp.float32),
            pltpu.VMEM((6, STRIP * 8, LANES), jnp.float32),
            pltpu.VMEM((waves_total // LANES, packed, LANES), jnp.float32),
        ],
        compiler_params=pltpu.CompilerParams(vmem_limit_bytes=60 * 2**20),
    )(
        band,
        depths,
        orders.astype(jnp.float32)[None],
        u,
        v,
        temp,
        oro,
    )
    devices = lev_count * wide_count
    slots = waves_total // devices
    got = exchange(coefs.reshape(devices, slots, packed), ("wide", "lev"), devices, 0)
    got = got[:, :, :6 * rows].astype(jnp.float32)
    got = got.reshape(wide_count, lev_count, slots, 3, 2, rows)
    under = got[:, :, :, 1]
    below = jnp.cumsum(under[:, ::-1], axis=1)[:, ::-1] - under
    fields = jnp.stack([got[:, :, :, 0] + below, got[:, :, :, 2]], axis=3)
    half = wide_count // 2
    upper = fields[:half]
    lower = fields[half:][::-1]
    both = jnp.stack([upper + lower, upper - lower], axis=0).astype(jnp.bfloat16)
    both = both.transpose(3, 0, 5, 2, 4, 1, 6)
    pairs = slots // 2
    width = table.shape[2]
    both = both.reshape(pairs, -1, half * rows)
    product = jnp.einsum("pkj,pjc->pkc", both, table, preferred_element_type=jnp.float32)
    product = product.reshape(pairs, 4, 2, lev_count, 2, width)
    mine = lax.dynamic_slice_in_dim(orders, (wide * lev_count + lev) * slots, slots)
    first = mine.reshape(pairs, 2)[:, :1]
    column = jnp.arange(width, dtype=jnp.int32)[None]
    split = waves_total - first
    chosen = jnp.where(column < split, column % 2, 2 + (column - split) % 2)
    chosen = jnp.where(column <= waves_total, chosen, 4)[:, None, None, None, :]
    result = jnp.zeros_like(product[:, 0])
    for k in range(4):
        result = jnp.where(chosen == k, product[:, k], result)
    return result.astype(jnp.bfloat16)


def solution(mesh):
    in_specs = (
        P("lev", "wide", None),
        P("lev", "wide", None),
        P("lev", "wide", None),
        P("wide", None),
        P(),
        P(("wide", "lev")),
        P(),
        P(("wide", "lev"), None, None),
    )
    out_specs = P(("wide", "lev"), None, None, None, None)
    return jax.shard_map(local, mesh=mesh, in_specs=in_specs, out_specs=out_specs, check_vma=False)
```

```python
import functools

import jax
import jax.numpy as jnp
from jax import lax
from jax.experimental import pallas as pl
from jax.experimental.pallas import tpu as pltpu
from jax.sharding import PartitionSpec as P

STRIP = 16
LANES = 128
COS = (0.9999992251396179, -19.738981246948242, 64.92865753173828, -85.27162170410156, 58.79049301147461, -21.07110595703125)
SIN = (6.283185005187988, -41.341590881347656, 81.59994506835938, -76.61447143554688, 41.3428840637207, -12.471243858337402)


def horner(coefs, z):
    value = jnp.full_like(z, coefs[-1])
    for c in coefs[-2::-1]:
        value = value * z + c
    return value


def unit(n, length, inverse):
    turns = jnp.round(n * inverse)
    t = (n - turns * length) * inverse
    z = t * t
    return horner(COS, z), t * horner(SIN, z)


def times(a, b):
    return a[0] * b[0] - a[1] * b[1], a[0] * b[1] + a[1] * b[0]


MESH = pl.DeviceIdType.MESH


def swap(axes, x, out, landed, send_sem, recv_sem):
    sizes = [lax.axis_size(a) for a in axes]
    count = 1
    me = 0
    for a, size in zip(axes, sizes):
        count = count * size
        me = me * size + lax.axis_index(a)
    shared = x.shape[0] != count

    def device(turn):
        peer = lax.rem(me + turn, count)
        if len(axes) == 1:
            return peer, {axes[0]: peer}
        return peer, {axes[0]: lax.div(peer, sizes[1]), axes[1]: lax.rem(peer, sizes[1])}

    barrier = pltpu.get_barrier_semaphore()

    def greet(turn, carry):
        pl.semaphore_signal(barrier, inc=1, device_id=device(turn)[1], device_id_type=MESH)
        return carry

    lax.fori_loop(1, count, greet, 0)
    pl.semaphore_wait(barrier, count - 1)

    def copy(turn):
        peer, where = device(turn)
        return pltpu.make_async_remote_copy(
            src_ref=x.at[0 if shared else peer],
            dst_ref=landed.at[me],
            send_sem=send_sem.at[turn],
            recv_sem=recv_sem.at[turn],
            device_id=where,
            device_id_type=MESH,
        )

    def begin(turn, carry):
        copy(turn).start()
        return carry

    def finish(turn, carry):
        copy(turn).wait()
        return carry

    lax.fori_loop(1, count, begin, 0)
    landed[me] = x[0 if shared else me]
    lax.fori_loop(1, count, finish, 0)
    out[...] = landed[...]


def exchange(x, axes, count, number):
    shape = (count,) + x.shape[1:]
    vmem = pl.BlockSpec(memory_space=pltpu.VMEM)
    return pl.pallas_call(
        functools.partial(swap, axes),
        out_shape=jax.ShapeDtypeStruct(shape, x.dtype),
        in_specs=[vmem],
        out_specs=vmem,
        scratch_shapes=[
            pltpu.VMEM(shape, x.dtype),
            pltpu.SemaphoreType.DMA((count,)),
            pltpu.SemaphoreType.DMA((count,)),
        ],
        compiler_params=pltpu.CompilerParams(
            collective_id=number, has_side_effects=True, vmem_limit_bytes=24 * 2**20
        ),
    )(x)


def transform(high, high_pad, lens, depths, waves, u, v, temp, oro, out, spread, sums, gathered):
    step = pl.program_id(0)
    steps = pl.num_programs(0)
    rows = steps * STRIP
    south = lax.axis_index("wide") * 2 >= lax.axis_size("wide")
    level = lax.axis_index("lev")
    depth = depths[level]
    ground = jnp.where(level == lax.axis_size("lev") - 1, 1.0, 0.0)
    share = rows // lens.shape[0]

    def row_length(r):
        row = step * STRIP + r
        return lens[lax.div(row, share), 0, lax.rem(row, share)]

    backward = lax.broadcasted_iota(jnp.int32, (STRIP, LANES), 0)
    limit = jnp.zeros((STRIP, LANES), jnp.int32)
    for r in range(STRIP):
        limit = jnp.where(backward == r, row_length(r), limit)
    lane = lax.broadcasted_iota(jnp.int32, (STRIP, LANES), 1)
    for h in range(high_pad):
        at = pl.ds(h * STRIP, STRIP)
        if h >= high:
            for c in range(3):
                spread[c, at, :] = jnp.zeros((STRIP, LANES), jnp.float32)
            continue
        cols = pl.ds(h * LANES, LANES)
        east = u[:, cols].astype(jnp.float32)
        north = v[:, cols].astype(jnp.float32)
        heat = temp[:, cols].astype(jnp.float32)
        weighted = heat * depth + oro[:, cols].astype(jnp.float32) * ground
        energy = 0.5 * (east * east + north * north) + weighted
        inside = lane + h * LANES < limit
        spread[0, at, :] = jnp.where(inside, energy, 0.0)
        spread[1, at, :] = jnp.where(inside, weighted, 0.0)
        spread[2, at, :] = jnp.where(inside, north * heat, 0.0)

    sub = lax.broadcasted_iota(jnp.int32, (8, LANES), 0).astype(jnp.float32)
    chunks = waves.shape[1] // LANES
    for chunk in range(chunks):
        m = jnp.broadcast_to(waves[:, chunk * LANES:(chunk + 1) * LANES], (8, LANES)).astype(jnp.float32)

        def one_row(r, carry):
            length = jnp.broadcast_to(row_length(r).astype(jnp.float32), (8, LANES))
            inverse = 1.0 / length
            data = jnp.concatenate(
                [spread[c, pl.ds(r, high_pad, stride=STRIP), :] for c in range(3)], axis=0
            ).astype(jnp.bfloat16)
            tiles = [unit(m * sub, length, inverse)]
            turn = unit(m * 8.0, length, inverse)
            while len(tiles) < LANES // 8:
                tiles = tiles + [times(tile, turn) for tile in tiles]
                turn = times(turn, turn)
            table = jnp.concatenate(
                [
                    jnp.concatenate([tile[0] for tile in tiles], axis=0),
                    jnp.concatenate([tile[1] for tile in tiles], axis=0),
                ],
                axis=1,
            ).astype(jnp.bfloat16)
            part = jnp.dot(data, table, preferred_element_type=jnp.float32)
            outer = [unit(m * (sub * float(LANES)), length, inverse)]
            stride = unit(m * float(8 * LANES), length, inverse)
            while len(outer) < high_pad // 8:
                outer.append(times(outer[-1], stride))
            place = jnp.where(south, STRIP - 1 - r, r)
            for c in range(3):
                real = jnp.zeros((8, LANES), jnp.float32)
                imag = jnp.zeros((8, LANES), jnp.float32)
                for g in range(high_pad // 8):
                    base = c * high_pad + g * 8
                    pc = part[base:base + 8, :LANES]
                    ps = part[base:base + 8, LANES:]
                    oc, os = outer[g]
                    real = real + (pc * oc - ps * os)
                    imag = imag - (pc * os + ps * oc)
                at = pl.ds(pl.multiple_of(place * 8, 8), 8)
                sums[2 * c, at, :] = real
                sums[2 * c + 1, at, :] = imag
            return carry

        lax.fori_loop(0, STRIP, one_row, 0, unroll=8)

        block = jnp.where(south, steps - 1 - step, step) * STRIP
        m16 = jnp.broadcast_to(
            waves[:, chunk * LANES:(chunk + 1) * LANES], (STRIP, LANES)
        ).astype(jnp.float32)
        length = jnp.zeros((STRIP, LANES), jnp.int32)
        for r in range(STRIP):
            place = jnp.where(south, STRIP - 1 - r, r)
            length = jnp.where(backward == place, row_length(r), length)
        length = length.astype(jnp.float32)
        factor = jnp.where(2.0 * m16 < length, 1.0 / length, 0.0)
        for k in range(6):
            total = sums[k, pl.ds(0, STRIP, stride=8), :]
            for s in range(1, 8):
                total = total + sums[k, pl.ds(s, STRIP, stride=8), :]
            at = pl.ds(pl.multiple_of(k * rows + block, STRIP), STRIP)
            gathered[chunk, at, :] = total * factor

    @pl.when(step == 0)
    def _():
        tail = gathered.shape[1] - 6 * rows
        if tail:
            for chunk in range(chunks):
                gathered[chunk, 6 * rows:, :] = jnp.zeros((tail, LANES), jnp.float32)

    @pl.when(step == steps - 1)
    def _():
        for chunk in range(chunks):
            for b in range(gathered.shape[1] // LANES):
                turned = gathered[chunk, b * LANES:(b + 1) * LANES, :].T.astype(out.dtype)
                slots = out.shape[1]
                owners = LANES // slots
                out[chunk * owners:(chunk + 1) * owners, :, b * LANES:(b + 1) * LANES] = (
                    turned.reshape(owners, slots, LANES)
                )


def local(u, v, temp, oro, depths, lens, orders, table):
    lev_count = lax.axis_size("lev")
    wide_count = lax.axis_size("wide")
    lev = lax.axis_index("lev")
    wide = lax.axis_index("wide")
    rows = temp.shape[1]
    samples = temp.shape[2]
    waves_total = orders.shape[0]
    high = samples // LANES
    high_pad = -(-high // 8) * 8
    steps = rows // STRIP
    devices = lev_count * wide_count
    slots = waves_total // devices
    packed = -(-6 * rows // LANES) * LANES
    held = lens.reshape(1, 1, lens.shape[0])
    band = exchange(held, ("lev",), lev_count, 1)
    smem = pl.BlockSpec(memory_space=pltpu.SMEM)
    field = pl.BlockSpec((STRIP, samples), lambda i: (i, 0))
    field3 = pl.BlockSpec((None, STRIP, samples), lambda i: (0, i, 0))
    coefs = pl.pallas_call(
        functools.partial(transform, high, high_pad),
        grid=(steps,),
        out_shape=jax.ShapeDtypeStruct((devices, slots, packed), jnp.bfloat16),
        in_specs=[
            smem,
            smem,
            pl.BlockSpec((1, waves_total), lambda i: (0, 0)),
            field3,
            field3,
            field3,
            field,
        ],
        out_specs=pl.BlockSpec((devices, slots, packed), lambda i: (0, 0, 0)),
        scratch_shapes=[
            pltpu.VMEM((3, high_pad * STRIP, LANES), jnp.float32),
            pltpu.VMEM((6, STRIP * 8, LANES), jnp.float32),
            pltpu.VMEM((waves_total // LANES, packed, LANES), jnp.float32),
        ],
        compiler_params=pltpu.CompilerParams(vmem_limit_bytes=60 * 2**20),
    )(
        band,
        depths,
        orders[None],
        u,
        v,
        temp,
        oro,
    )
    got = exchange(coefs, ("wide", "lev"), devices, 0)
    got = got[:, :, :6 * rows].astype(jnp.float32)
    got = got.reshape(wide_count, lev_count, slots, 3, 2, rows)
    under = got[:, :, :, 1]
    below = jnp.cumsum(under[:, ::-1], axis=1)[:, ::-1] - under
    fields = jnp.stack([got[:, :, :, 0] + below, got[:, :, :, 2]], axis=3)
    half = wide_count // 2
    upper = fields[:half]
    lower = fields[half:][::-1]
    both = jnp.stack([upper + lower, upper - lower], axis=0).astype(jnp.bfloat16)
    both = both.transpose(3, 0, 5, 2, 4, 1, 6)
    pairs = slots // 2
    width = table.shape[2]
    both = both.reshape(pairs, -1, half * rows)
    product = jnp.einsum("pkj,pjc->pkc", both, table, preferred_element_type=jnp.float32)
    product = product.reshape(pairs, 4, 2, lev_count, 2, width)
    mine = lax.dynamic_slice_in_dim(orders, (wide * lev_count + lev) * slots, slots)
    first = mine.reshape(pairs, 2)[:, :1]
    column = jnp.arange(width, dtype=jnp.int32)[None]
    split = waves_total - first
    chosen = jnp.where(column < split, column % 2, 2 + (column - split) % 2)
    chosen = jnp.where(column <= waves_total, chosen, 4)[:, None, None, None, :]
    result = jnp.zeros_like(product[:, 0])
    for k in range(4):
        result = jnp.where(chosen == k, product[:, k], result)
    return result.astype(jnp.bfloat16)


def solution(mesh):
    in_specs = (
        P("lev", "wide", None),
        P("lev", "wide", None),
        P("lev", "wide", None),
        P("wide", None),
        P(),
        P(("wide", "lev")),
        P(),
        P(("wide", "lev"), None, None),
    )
    out_specs = P(("wide", "lev"), None, None, None, None)
    return jax.shard_map(local, mesh=mesh, in_specs=in_specs, out_specs=out_specs, check_vma=False)
```

```python
import functools

import jax
import jax.numpy as jnp
from jax import lax
from jax.experimental import pallas as pl
from jax.experimental.pallas import tpu as pltpu
from jax.sharding import PartitionSpec as P

STRIP = 16
LANES = 128
COS = (0.9999992251396179, -19.738981246948242, 64.92865753173828, -85.27162170410156, 58.79049301147461, -21.07110595703125)
SIN = (6.283185005187988, -41.341590881347656, 81.59994506835938, -76.61447143554688, 41.3428840637207, -12.471243858337402)


def horner(coefs, z):
    value = jnp.full_like(z, coefs[-1])
    for c in coefs[-2::-1]:
        value = value * z + c
    return value


def unit(n, length, inverse):
    turns = jnp.round(n * inverse)
    t = (n - turns * length) * inverse
    z = t * t
    return horner(COS, z), t * horner(SIN, z)


def times(a, b):
    return a[0] * b[0] - a[1] * b[1], a[0] * b[1] + a[1] * b[0]


MESH = pl.DeviceIdType.MESH


def swap(axes, x, out, landed, send_sem, recv_sem):
    sizes = [lax.axis_size(a) for a in axes]
    count = 1
    me = 0
    for a, size in zip(axes, sizes):
        count = count * size
        me = me * size + lax.axis_index(a)
    shared = x.shape[0] != count

    def device(turn):
        peer = lax.rem(me + turn, count)
        if len(axes) == 1:
            return peer, {axes[0]: peer}
        return peer, {axes[0]: lax.div(peer, sizes[1]), axes[1]: lax.rem(peer, sizes[1])}

    barrier = pltpu.get_barrier_semaphore()

    def greet(turn, carry):
        pl.semaphore_signal(barrier, inc=1, device_id=device(turn)[1], device_id_type=MESH)
        return carry

    lax.fori_loop(1, count, greet, 0)
    pl.semaphore_wait(barrier, count - 1)

    def copy(turn):
        peer, where = device(turn)
        return pltpu.make_async_remote_copy(
            src_ref=x.at[0 if shared else peer],
            dst_ref=landed.at[me],
            send_sem=send_sem.at[turn],
            recv_sem=recv_sem.at[turn],
            device_id=where,
            device_id_type=MESH,
        )

    def begin(turn, carry):
        copy(turn).start()
        return carry

    def finish(turn, carry):
        copy(turn).wait()
        return carry

    lax.fori_loop(1, count, begin, 0)
    landed[me] = x[0 if shared else me]
    lax.fori_loop(1, count, finish, 0)
    out[...] = landed[...]


def exchange(x, axes, count, number):
    shape = (count,) + x.shape[1:]
    vmem = pl.BlockSpec(memory_space=pltpu.VMEM)
    return pl.pallas_call(
        functools.partial(swap, axes),
        out_shape=jax.ShapeDtypeStruct(shape, x.dtype),
        in_specs=[vmem],
        out_specs=vmem,
        scratch_shapes=[
            pltpu.VMEM(shape, x.dtype),
            pltpu.SemaphoreType.DMA((count,)),
            pltpu.SemaphoreType.DMA((count,)),
        ],
        compiler_params=pltpu.CompilerParams(
            collective_id=number, has_side_effects=True, vmem_limit_bytes=24 * 2**20
        ),
    )(x)


def transform(high, high_pad, lens, depths, waves, u, v, temp, oro, out, spread, sums, gathered):
    step = pl.program_id(0)
    steps = pl.num_programs(0)
    rows = steps * STRIP
    south = lax.axis_index("wide") * 2 >= lax.axis_size("wide")
    level = lax.axis_index("lev")
    depth = depths[level]
    ground = jnp.where(level == lax.axis_size("lev") - 1, 1.0, 0.0)
    share = rows // lens.shape[0]

    def row_length(r):
        row = step * STRIP + r
        return lens[lax.div(row, share), 0, lax.rem(row, share)]

    backward = lax.broadcasted_iota(jnp.int32, (STRIP, LANES), 0)
    limit = jnp.zeros((STRIP, LANES), jnp.int32)
    for r in range(STRIP):
        limit = jnp.where(backward == r, row_length(r), limit)
    lane = lax.broadcasted_iota(jnp.int32, (STRIP, LANES), 1)
    for h in range(high_pad):
        at = pl.ds(h * STRIP, STRIP)
        if h >= high:
            for c in range(3):
                spread[c, at, :] = jnp.zeros((STRIP, LANES), jnp.float32)
            continue
        cols = pl.ds(h * LANES, LANES)
        east = u[:, cols].astype(jnp.float32)
        north = v[:, cols].astype(jnp.float32)
        heat = temp[:, cols].astype(jnp.float32)
        weighted = heat * depth + oro[:, cols].astype(jnp.float32) * ground
        energy = 0.5 * (east * east + north * north) + weighted
        inside = lane + h * LANES < limit
        spread[0, at, :] = jnp.where(inside, energy, 0.0)
        spread[1, at, :] = jnp.where(inside, weighted, 0.0)
        spread[2, at, :] = jnp.where(inside, north * heat, 0.0)

    sub = lax.broadcasted_iota(jnp.int32, (8, LANES), 0).astype(jnp.float32)
    chunks = waves.shape[1] // LANES
    for chunk in range(chunks):
        m = jnp.broadcast_to(waves[:, chunk * LANES:(chunk + 1) * LANES], (8, LANES)).astype(jnp.float32)

        def one_row(r, carry):
            length = jnp.broadcast_to(row_length(r).astype(jnp.float32), (8, LANES))
            inverse = 1.0 / length
            data = jnp.concatenate(
                [spread[c, pl.ds(r, high_pad, stride=STRIP), :] for c in range(3)], axis=0
            ).astype(jnp.bfloat16)
            tiles = [unit(m * sub, length, inverse)]
            turn = unit(m * 8.0, length, inverse)
            while len(tiles) < LANES // 8:
                tiles = tiles + [times(tile, turn) for tile in tiles]
                turn = times(turn, turn)
            table = jnp.concatenate(
                [
                    jnp.concatenate([tile[0] for tile in tiles], axis=0),
                    jnp.concatenate([tile[1] for tile in tiles], axis=0),
                ],
                axis=1,
            ).astype(jnp.bfloat16)
            part = jnp.dot(data, table, preferred_element_type=jnp.float32)
            outer = [unit(m * (sub * float(LANES)), length, inverse)]
            stride = unit(m * float(8 * LANES), length, inverse)
            while len(outer) < high_pad // 8:
                outer.append(times(outer[-1], stride))
            place = jnp.where(south, STRIP - 1 - r, r)
            for c in range(3):
                real = jnp.zeros((8, LANES), jnp.float32)
                imag = jnp.zeros((8, LANES), jnp.float32)
                for g in range(high_pad // 8):
                    base = c * high_pad + g * 8
                    pc = part[base:base + 8, :LANES]
                    ps = part[base:base + 8, LANES:]
                    oc, os = outer[g]
                    real = real + (pc * oc - ps * os)
                    imag = imag - (pc * os + ps * oc)
                at = pl.ds(pl.multiple_of(place * 8, 8), 8)
                sums[2 * c, at, :] = real
                sums[2 * c + 1, at, :] = imag
            return carry

        lax.fori_loop(0, STRIP, one_row, 0, unroll=16)

        block = jnp.where(south, steps - 1 - step, step) * STRIP
        m16 = jnp.broadcast_to(
            waves[:, chunk * LANES:(chunk + 1) * LANES], (STRIP, LANES)
        ).astype(jnp.float32)
        length = jnp.zeros((STRIP, LANES), jnp.int32)
        for r in range(STRIP):
            place = jnp.where(south, STRIP - 1 - r, r)
            length = jnp.where(backward == place, row_length(r), length)
        length = length.astype(jnp.float32)
        factor = jnp.where(2.0 * m16 < length, 1.0 / length, 0.0)
        for k in range(6):
            total = sums[k, pl.ds(0, STRIP, stride=8), :]
            for s in range(1, 8):
                total = total + sums[k, pl.ds(s, STRIP, stride=8), :]
            at = pl.ds(pl.multiple_of(k * rows + block, STRIP), STRIP)
            gathered[chunk, at, :] = total * factor

    @pl.when(step == 0)
    def _():
        tail = gathered.shape[1] - 6 * rows
        if tail:
            for chunk in range(chunks):
                gathered[chunk, 6 * rows:, :] = jnp.zeros((tail, LANES), jnp.float32)

    @pl.when(step == steps - 1)
    def _():
        for chunk in range(chunks):
            for b in range(gathered.shape[1] // LANES):
                turned = gathered[chunk, b * LANES:(b + 1) * LANES, :].T.astype(out.dtype)
                slots = out.shape[1]
                owners = LANES // slots
                out[chunk * owners:(chunk + 1) * owners, :, b * LANES:(b + 1) * LANES] = (
                    turned.reshape(owners, slots, LANES)
                )


def local(u, v, temp, oro, depths, lens, orders, table):
    lev_count = lax.axis_size("lev")
    wide_count = lax.axis_size("wide")
    lev = lax.axis_index("lev")
    wide = lax.axis_index("wide")
    rows = temp.shape[1]
    samples = temp.shape[2]
    waves_total = orders.shape[0]
    high = samples // LANES
    high_pad = -(-high // 8) * 8
    steps = rows // STRIP
    devices = lev_count * wide_count
    slots = waves_total // devices
    packed = -(-6 * rows // LANES) * LANES
    held = lens.reshape(1, 1, lens.shape[0])
    band = exchange(held, ("lev",), lev_count, 1)
    smem = pl.BlockSpec(memory_space=pltpu.SMEM)
    field = pl.BlockSpec((STRIP, samples), lambda i: (i, 0))
    field3 = pl.BlockSpec((None, STRIP, samples), lambda i: (0, i, 0))
    coefs = pl.pallas_call(
        functools.partial(transform, high, high_pad),
        grid=(steps,),
        out_shape=jax.ShapeDtypeStruct((devices, slots, packed), jnp.bfloat16),
        in_specs=[
            smem,
            smem,
            pl.BlockSpec((1, waves_total), lambda i: (0, 0)),
            field3,
            field3,
            field3,
            field,
        ],
        out_specs=pl.BlockSpec((devices, slots, packed), lambda i: (0, 0, 0)),
        scratch_shapes=[
            pltpu.VMEM((3, high_pad * STRIP, LANES), jnp.float32),
            pltpu.VMEM((6, STRIP * 8, LANES), jnp.float32),
            pltpu.VMEM((waves_total // LANES, packed, LANES), jnp.float32),
        ],
        compiler_params=pltpu.CompilerParams(vmem_limit_bytes=60 * 2**20),
    )(
        band,
        depths,
        orders[None],
        u,
        v,
        temp,
        oro,
    )
    got = exchange(coefs, ("wide", "lev"), devices, 0)
    got = got[:, :, :6 * rows].astype(jnp.float32)
    got = got.reshape(wide_count, lev_count, slots, 3, 2, rows)
    under = got[:, :, :, 1]
    below = jnp.cumsum(under[:, ::-1], axis=1)[:, ::-1] - under
    fields = jnp.stack([got[:, :, :, 0] + below, got[:, :, :, 2]], axis=3)
    half = wide_count // 2
    upper = fields[:half]
    lower = fields[half:][::-1]
    both = jnp.stack([upper + lower, upper - lower], axis=0).astype(jnp.bfloat16)
    both = both.transpose(3, 0, 5, 2, 4, 1, 6)
    pairs = slots // 2
    width = table.shape[2]
    both = both.reshape(pairs, -1, half * rows)
    product = jnp.einsum("pkj,pjc->pkc", both, table, preferred_element_type=jnp.float32)
    product = product.reshape(pairs, 4, 2, lev_count, 2, width)
    mine = lax.dynamic_slice_in_dim(orders, (wide * lev_count + lev) * slots, slots)
    first = mine.reshape(pairs, 2)[:, :1]
    column = jnp.arange(width, dtype=jnp.int32)[None]
    split = waves_total - first
    chosen = jnp.where(column < split, column % 2, 2 + (column - split) % 2)
    chosen = jnp.where(column <= waves_total, chosen, 4)[:, None, None, None, :]
    result = jnp.zeros_like(product[:, 0])
    for k in range(4):
        result = jnp.where(chosen == k, product[:, k], result)
    return result.astype(jnp.bfloat16)


def solution(mesh):
    in_specs = (
        P("lev", "wide", None),
        P("lev", "wide", None),
        P("lev", "wide", None),
        P("wide", None),
        P(),
        P(("wide", "lev")),
        P(),
        P(("wide", "lev"), None, None),
    )
    out_specs = P(("wide", "lev"), None, None, None, None)
    return jax.shard_map(local, mesh=mesh, in_specs=in_specs, out_specs=out_specs, check_vma=False)
```

```python
import functools

import jax
import jax.numpy as jnp
from jax import lax
from jax.experimental import pallas as pl
from jax.experimental.pallas import tpu as pltpu
from jax.sharding import PartitionSpec as P

STRIP = 16
LANES = 128
COS = (0.9999992251396179, -19.738981246948242, 64.92865753173828, -85.27162170410156, 58.79049301147461, -21.07110595703125)
SIN = (6.283185005187988, -41.341590881347656, 81.59994506835938, -76.61447143554688, 41.3428840637207, -12.471243858337402)


def horner(coefs, z):
    value = jnp.full_like(z, coefs[-1])
    for c in coefs[-2::-1]:
        value = value * z + c
    return value


def unit(n, length, inverse):
    turns = jnp.round(n * inverse)
    t = (n - turns * length) * inverse
    z = t * t
    return horner(COS, z), t * horner(SIN, z)


def times(a, b):
    return a[0] * b[0] - a[1] * b[1], a[0] * b[1] + a[1] * b[0]


MESH = pl.DeviceIdType.MESH


def swap(axes, x, out, landed, send_sem, recv_sem):
    sizes = [lax.axis_size(a) for a in axes]
    count = 1
    me = 0
    for a, size in zip(axes, sizes):
        count = count * size
        me = me * size + lax.axis_index(a)
    shared = x.shape[0] != count

    def device(turn):
        peer = lax.rem(me + turn, count)
        if len(axes) == 1:
            return peer, {axes[0]: peer}
        return peer, {axes[0]: lax.div(peer, sizes[1]), axes[1]: lax.rem(peer, sizes[1])}

    barrier = pltpu.get_barrier_semaphore()

    def greet(turn, carry):
        pl.semaphore_signal(barrier, inc=1, device_id=device(turn)[1], device_id_type=MESH)
        return carry

    lax.fori_loop(1, count, greet, 0)
    pl.semaphore_wait(barrier, count - 1)

    def copy(turn):
        peer, where = device(turn)
        return pltpu.make_async_remote_copy(
            src_ref=x.at[0 if shared else peer],
            dst_ref=landed.at[me],
            send_sem=send_sem.at[turn],
            recv_sem=recv_sem.at[turn],
            device_id=where,
            device_id_type=MESH,
        )

    def begin(turn, carry):
        copy(turn).start()
        return carry

    def finish(turn, carry):
        copy(turn).wait()
        return carry

    lax.fori_loop(1, count, begin, 0)
    landed[me] = x[0 if shared else me]
    lax.fori_loop(1, count, finish, 0)
    out[...] = landed[...]


def exchange(x, axes, count, number):
    shape = (count,) + x.shape[1:]
    vmem = pl.BlockSpec(memory_space=pltpu.VMEM)
    return pl.pallas_call(
        functools.partial(swap, axes),
        out_shape=jax.ShapeDtypeStruct(shape, x.dtype),
        in_specs=[vmem],
        out_specs=vmem,
        scratch_shapes=[
            pltpu.VMEM(shape, x.dtype),
            pltpu.SemaphoreType.DMA((count,)),
            pltpu.SemaphoreType.DMA((count,)),
        ],
        compiler_params=pltpu.CompilerParams(
            collective_id=number, has_side_effects=True, vmem_limit_bytes=24 * 2**20
        ),
    )(x)


def transform(high, high_pad, lens, depths, waves, u, v, temp, oro, out, spread, sums, gathered):
    step = pl.program_id(0)
    steps = pl.num_programs(0)
    rows = steps * STRIP
    south = lax.axis_index("wide") * 2 >= lax.axis_size("wide")
    level = lax.axis_index("lev")
    depth = depths[level]
    ground = jnp.where(level == lax.axis_size("lev") - 1, 1.0, 0.0)
    share = rows // lens.shape[0]

    def row_length(r):
        row = step * STRIP + r
        return lens[lax.div(row, share), 0, lax.rem(row, share)]

    backward = lax.broadcasted_iota(jnp.int32, (STRIP, LANES), 0)
    limit = jnp.zeros((STRIP, LANES), jnp.int32)
    for r in range(STRIP):
        limit = jnp.where(backward == r, row_length(r), limit)
    lane = lax.broadcasted_iota(jnp.int32, (STRIP, LANES), 1)
    for h in range(high_pad):
        at = pl.ds(h * STRIP, STRIP)
        if h >= high:
            for c in range(3):
                spread[c, at, :] = jnp.zeros((STRIP, LANES), jnp.float32)
            continue
        cols = pl.ds(h * LANES, LANES)
        east = u[:, cols].astype(jnp.float32)
        north = v[:, cols].astype(jnp.float32)
        heat = temp[:, cols].astype(jnp.float32)
        weighted = heat * depth + oro[:, cols].astype(jnp.float32) * ground
        energy = 0.5 * (east * east + north * north) + weighted
        inside = lane + h * LANES < limit
        spread[0, at, :] = jnp.where(inside, energy, 0.0)
        spread[1, at, :] = jnp.where(inside, weighted, 0.0)
        spread[2, at, :] = jnp.where(inside, north * heat, 0.0)

    sub = lax.broadcasted_iota(jnp.int32, (8, LANES), 0).astype(jnp.float32)
    chunks = waves.shape[1] // LANES
    for chunk in range(chunks):
        m = jnp.broadcast_to(waves[:, chunk * LANES:(chunk + 1) * LANES], (8, LANES)).astype(jnp.float32)

        def one_row(r, carry):
            length = jnp.broadcast_to(row_length(r).astype(jnp.float32), (8, LANES))
            inverse = 1.0 / length
            data = jnp.concatenate(
                [spread[c, pl.ds(r, high_pad, stride=STRIP), :] for c in range(3)], axis=0
            ).astype(jnp.bfloat16)
            tiles = [unit(m * sub, length, inverse)]
            turn = unit(m * 8.0, length, inverse)
            while len(tiles) < LANES // 8:
                tiles = tiles + [times(tile, turn) for tile in tiles]
                turn = times(turn, turn)
            table = jnp.concatenate(
                [
                    jnp.concatenate([tile[0] for tile in tiles], axis=0),
                    jnp.concatenate([tile[1] for tile in tiles], axis=0),
                ],
                axis=1,
            ).astype(jnp.bfloat16)
            part = jnp.dot(data, table, preferred_element_type=jnp.float32)
            outer = [unit(m * (sub * float(LANES)), length, inverse)]
            stride = unit(m * float(8 * LANES), length, inverse)
            while len(outer) < high_pad // 8:
                outer.append(times(outer[-1], stride))
            place = jnp.where(south, STRIP - 1 - r, r)
            for c in range(3):
                real = jnp.zeros((8, LANES), jnp.float32)
                imag = jnp.zeros((8, LANES), jnp.float32)
                for g in range(high_pad // 8):
                    base = c * high_pad + g * 8
                    pc = part[base:base + 8, :LANES]
                    ps = part[base:base + 8, LANES:]
                    oc, os = outer[g]
                    real = real + (pc * oc - ps * os)
                    imag = imag - (pc * os + ps * oc)
                at = pl.ds(pl.multiple_of(place * 8, 8), 8)
                sums[2 * c, at, :] = real
                sums[2 * c + 1, at, :] = imag
            return carry

        lax.fori_loop(0, STRIP, one_row, 0, unroll=8)

        block = jnp.where(south, steps - 1 - step, step) * STRIP
        m16 = jnp.broadcast_to(
            waves[:, chunk * LANES:(chunk + 1) * LANES], (STRIP, LANES)
        ).astype(jnp.float32)
        length = jnp.zeros((STRIP, LANES), jnp.int32)
        for r in range(STRIP):
            place = jnp.where(south, STRIP - 1 - r, r)
            length = jnp.where(backward == place, row_length(r), length)
        length = length.astype(jnp.float32)
        factor = jnp.where(2.0 * m16 < length, 1.0 / length, 0.0)
        for k in range(6):
            total = sums[k, pl.ds(0, STRIP, stride=8), :]
            for s in range(1, 8):
                total = total + sums[k, pl.ds(s, STRIP, stride=8), :]
            at = pl.ds(pl.multiple_of(k * rows + block, STRIP), STRIP)
            gathered[chunk, at, :] = total * factor

    @pl.when(step == 0)
    def _():
        tail = gathered.shape[1] - 6 * rows
        if tail:
            for chunk in range(chunks):
                gathered[chunk, 6 * rows:, :] = jnp.zeros((tail, LANES), jnp.float32)

    @pl.when(step == steps - 1)
    def _():
        for chunk in range(chunks):
            for b in range(gathered.shape[1] // LANES):
                turned = gathered[chunk, b * LANES:(b + 1) * LANES, :].T.astype(out.dtype)
                slots = out.shape[1]
                owners = LANES // slots
                out[chunk * owners:(chunk + 1) * owners, :, b * LANES:(b + 1) * LANES] = (
                    turned.reshape(owners, slots, LANES)
                )


def legendre(rows, waves_total, orders, got, table, out, first_kept, second_kept):
    levels = lax.axis_size("lev")
    bands = lax.axis_size("wide")
    slots = got.shape[1]
    device = lax.axis_index("wide") * levels + lax.axis_index("lev")
    half = bands // 2
    tall = levels * slots

    def band_fields(w):
        parts = [got[w * levels + l].astype(jnp.float32) for l in range(levels)]
        under = jnp.zeros((slots, 2 * rows), jnp.float32)
        energy = []
        for l in reversed(range(levels)):
            energy.append(parts[l][:, :2 * rows] + under)
            under = under + parts[l][:, 2 * rows:4 * rows]
        energy = jnp.concatenate(energy[::-1], axis=0)
        flux = jnp.concatenate([p[:, 4 * rows:6 * rows] for p in parts], axis=0)
        both = jnp.concatenate([energy, flux], axis=0)
        return jnp.concatenate([both[:, :rows], both[:, rows:]], axis=0)

    lefts = []
    for w in range(half):
        north = band_fields(w)
        south = band_fields(bands - 1 - w)
        lefts.append(jnp.concatenate([north + south, north - south], axis=0).astype(jnp.bfloat16))
    deep = 4 * tall
    for q in range(slots // 2):
        first = orders[device * slots + 2 * q]
        split = waves_total - first
        for chunk in range(table.shape[2] // LANES):
            cols = slice(chunk * LANES, (chunk + 1) * LANES)
            total = jnp.zeros((2 * deep, LANES), jnp.float32)
            for w in range(half):
                total = total + jnp.dot(
                    lefts[w],
                    table[q, w * rows:(w + 1) * rows, cols],
                    preferred_element_type=jnp.float32,
                )
            even = total[:deep]
            odd = total[deep:]
            column = lax.broadcasted_iota(jnp.int32, (deep, LANES), 1) + chunk * LANES
            shifted = column + split
            first_kept[...] = jnp.where((column & 1) == 0, even, odd)
            second_kept[...] = jnp.where((shifted & 1) == 0, even, odd)
            one = first_kept[pl.ds(2 * q, 4 * levels, stride=slots), :]
            two = second_kept[pl.ds(2 * q + 1, 4 * levels, stride=slots), :]
            column = lax.broadcasted_iota(jnp.int32, one.shape, 1) + chunk * LANES
            result = jnp.where(column < split, one, two)
            result = jnp.where(column <= waves_total, result, 0.0)
            out[q, :, cols] = result.astype(out.dtype)


def local(u, v, temp, oro, depths, lens, orders, table):
    lev_count = lax.axis_size("lev")
    wide_count = lax.axis_size("wide")
    lev = lax.axis_index("lev")
    wide = lax.axis_index("wide")
    rows = temp.shape[1]
    samples = temp.shape[2]
    waves_total = orders.shape[0]
    high = samples // LANES
    high_pad = -(-high // 8) * 8
    steps = rows // STRIP
    devices = lev_count * wide_count
    slots = waves_total // devices
    packed = -(-6 * rows // LANES) * LANES
    held = lens.reshape(1, 1, lens.shape[0])
    band = exchange(held, ("lev",), lev_count, 1)
    smem = pl.BlockSpec(memory_space=pltpu.SMEM)
    field = pl.BlockSpec((STRIP, samples), lambda i: (i, 0))
    field3 = pl.BlockSpec((None, STRIP, samples), lambda i: (0, i, 0))
    coefs = pl.pallas_call(
        functools.partial(transform, high, high_pad),
        grid=(steps,),
        out_shape=jax.ShapeDtypeStruct((devices, slots, packed), jnp.bfloat16),
        in_specs=[
            smem,
            smem,
            pl.BlockSpec((1, waves_total), lambda i: (0, 0)),
            field3,
            field3,
            field3,
            field,
        ],
        out_specs=pl.BlockSpec((devices, slots, packed), lambda i: (0, 0, 0)),
        scratch_shapes=[
            pltpu.VMEM((3, high_pad * STRIP, LANES), jnp.float32),
            pltpu.VMEM((6, STRIP * 8, LANES), jnp.float32),
            pltpu.VMEM((waves_total // LANES, packed, LANES), jnp.float32),
        ],
        compiler_params=pltpu.CompilerParams(vmem_limit_bytes=60 * 2**20),
    )(
        band,
        depths,
        orders[None],
        u,
        v,
        temp,
        oro,
    )
    got = exchange(coefs, ("wide", "lev"), devices, 0)
    pairs = slots // 2
    width = table.shape[2]
    vmem = pl.BlockSpec(memory_space=pltpu.VMEM)
    kept = pltpu.VMEM((4 * lev_count * slots, LANES), jnp.float32)
    result = pl.pallas_call(
        functools.partial(legendre, rows, waves_total),
        out_shape=jax.ShapeDtypeStruct((pairs, 4 * lev_count, width), jnp.bfloat16),
        in_specs=[smem, vmem, vmem],
        out_specs=vmem,
        scratch_shapes=[kept, kept],
        compiler_params=pltpu.CompilerParams(vmem_limit_bytes=40 * 2**20),
    )(orders, got, table)
    return result.reshape(pairs, 2, 2, lev_count, width).transpose(0, 1, 3, 2, 4)


def solution(mesh):
    in_specs = (
        P("lev", "wide", None),
        P("lev", "wide", None),
        P("lev", "wide", None),
        P("wide", None),
        P(),
        P(("wide", "lev")),
        P(),
        P(("wide", "lev"), None, None),
    )
    out_specs = P(("wide", "lev"), None, None, None, None)
    return jax.shard_map(local, mesh=mesh, in_specs=in_specs, out_specs=out_specs, check_vma=False)
```

```python
import functools

import jax
import jax.numpy as jnp
from jax import lax
from jax.experimental import pallas as pl
from jax.experimental.pallas import tpu as pltpu
from jax.sharding import PartitionSpec as P

STRIP = 16
LANES = 128
COS = (0.9999992251396179, -19.738981246948242, 64.92865753173828, -85.27162170410156, 58.79049301147461, -21.07110595703125)
SIN = (6.283185005187988, -41.341590881347656, 81.59994506835938, -76.61447143554688, 41.3428840637207, -12.471243858337402)


def horner(coefs, z):
    value = jnp.full_like(z, coefs[-1])
    for c in coefs[-2::-1]:
        value = value * z + c
    return value


def unit(n, length, inverse):
    turns = jnp.round(n * inverse)
    t = (n - turns * length) * inverse
    z = t * t
    return horner(COS, z), t * horner(SIN, z)


def times(a, b):
    return a[0] * b[0] - a[1] * b[1], a[0] * b[1] + a[1] * b[0]


MESH = pl.DeviceIdType.MESH


def swap(axes, x, out, landed, send_sem, recv_sem):
    sizes = [lax.axis_size(a) for a in axes]
    count = 1
    me = 0
    for a, size in zip(axes, sizes):
        count = count * size
        me = me * size + lax.axis_index(a)
    shared = x.shape[0] != count

    def device(turn):
        peer = lax.rem(me + turn, count)
        if len(axes) == 1:
            return peer, {axes[0]: peer}
        return peer, {axes[0]: lax.div(peer, sizes[1]), axes[1]: lax.rem(peer, sizes[1])}

    barrier = pltpu.get_barrier_semaphore()

    def greet(turn, carry):
        pl.semaphore_signal(barrier, inc=1, device_id=device(turn)[1], device_id_type=MESH)
        return carry

    lax.fori_loop(1, count, greet, 0)
    pl.semaphore_wait(barrier, count - 1)

    def copy(turn):
        peer, where = device(turn)
        return pltpu.make_async_remote_copy(
            src_ref=x.at[0 if shared else peer],
            dst_ref=landed.at[me],
            send_sem=send_sem.at[turn],
            recv_sem=recv_sem.at[turn],
            device_id=where,
            device_id_type=MESH,
        )

    def begin(step, carry):
        copy(1 + lax.rem(step + count // 2 - 1, count - 1)).start()
        return carry

    def finish(turn, carry):
        copy(turn).wait()
        return carry

    lax.fori_loop(0, count - 1, begin, 0)
    own = pltpu.make_async_copy(x.at[0 if shared else me], landed.at[me], send_sem.at[0])
    own.start()
    lax.fori_loop(1, count, finish, 0)
    own.wait()
    out[...] = landed[...]


def exchange(x, axes, count, number):
    shape = (count,) + x.shape[1:]
    vmem = pl.BlockSpec(memory_space=pltpu.VMEM)
    return pl.pallas_call(
        functools.partial(swap, axes),
        out_shape=jax.ShapeDtypeStruct(shape, x.dtype),
        in_specs=[pl.BlockSpec(memory_space=pl.ANY)],
        out_specs=vmem,
        scratch_shapes=[
            pltpu.VMEM(shape, x.dtype),
            pltpu.SemaphoreType.DMA((count,)),
            pltpu.SemaphoreType.DMA((count,)),
        ],
        compiler_params=pltpu.CompilerParams(
            collective_id=number, has_side_effects=True, vmem_limit_bytes=60 * 2**20
        ),
    )(x)


def transform(high, high_pad, lens, depths, waves, u, v, temp, oro, out, spread, sums, gathered):
    step = pl.program_id(0)
    steps = pl.num_programs(0)
    rows = steps * STRIP
    south = lax.axis_index("wide") * 2 >= lax.axis_size("wide")
    level = lax.axis_index("lev")
    depth = depths[level]
    ground = jnp.where(level == lax.axis_size("lev") - 1, 1.0, 0.0)
    share = rows // lens.shape[0]

    def row_length(r):
        row = step * STRIP + r
        return lens[lax.div(row, share), 0, lax.rem(row, share)]

    backward = lax.broadcasted_iota(jnp.int32, (STRIP, LANES), 0)
    limit = jnp.zeros((STRIP, LANES), jnp.int32)
    for r in range(STRIP):
        limit = jnp.where(backward == r, row_length(r), limit)
    lane = lax.broadcasted_iota(jnp.int32, (STRIP, LANES), 1)
    for h in range(high_pad):
        at = pl.ds(h * STRIP, STRIP)
        if h >= high:
            for c in range(3):
                spread[c, at, :] = jnp.zeros((STRIP, LANES), jnp.float32)
            continue
        cols = pl.ds(h * LANES, LANES)
        east = u[:, cols].astype(jnp.float32)
        north = v[:, cols].astype(jnp.float32)
        heat = temp[:, cols].astype(jnp.float32)
        weighted = heat * depth + oro[:, cols].astype(jnp.float32) * ground
        energy = 0.5 * (east * east + north * north) + weighted
        inside = lane + h * LANES < limit
        spread[0, at, :] = jnp.where(inside, energy, 0.0)
        spread[1, at, :] = jnp.where(inside, weighted, 0.0)
        spread[2, at, :] = jnp.where(inside, north * heat, 0.0)

    sub = lax.broadcasted_iota(jnp.int32, (8, LANES), 0).astype(jnp.float32)
    chunks = waves.shape[1] // LANES
    for chunk in range(chunks):
        m = jnp.broadcast_to(waves[:, chunk * LANES:(chunk + 1) * LANES], (8, LANES)).astype(jnp.float32)

        def one_row(r, carry):
            length = jnp.broadcast_to(row_length(r).astype(jnp.float32), (8, LANES))
            inverse = 1.0 / length
            data = jnp.concatenate(
                [spread[c, pl.ds(r, high_pad, stride=STRIP), :] for c in range(3)], axis=0
            ).astype(jnp.bfloat16)
            tiles = [unit(m * sub, length, inverse)]
            turn = unit(m * 8.0, length, inverse)
            while len(tiles) < LANES // 8:
                tiles = tiles + [times(tile, turn) for tile in tiles]
                turn = times(turn, turn)
            table = jnp.concatenate(
                [
                    jnp.concatenate([tile[0] for tile in tiles], axis=0),
                    jnp.concatenate([tile[1] for tile in tiles], axis=0),
                ],
                axis=1,
            ).astype(jnp.bfloat16)
            part = jnp.dot(data, table, preferred_element_type=jnp.float32)
            outer = [unit(m * (sub * float(LANES)), length, inverse)]
            stride = unit(m * float(8 * LANES), length, inverse)
            while len(outer) < high_pad // 8:
                outer.append(times(outer[-1], stride))
            place = jnp.where(south, STRIP - 1 - r, r)
            for c in range(3):
                real = jnp.zeros((8, LANES), jnp.float32)
                imag = jnp.zeros((8, LANES), jnp.float32)
                for g in range(high_pad // 8):
                    base = c * high_pad + g * 8
                    pc = part[base:base + 8, :LANES]
                    ps = part[base:base + 8, LANES:]
                    oc, os = outer[g]
                    real = real + (pc * oc - ps * os)
                    imag = imag - (pc * os + ps * oc)
                at = pl.ds(pl.multiple_of(place * 8, 8), 8)
                sums[2 * c, at, :] = real
                sums[2 * c + 1, at, :] = imag
            return carry

        lax.fori_loop(0, STRIP, one_row, 0, unroll=8)

        block = jnp.where(south, steps - 1 - step, step) * STRIP
        m16 = jnp.broadcast_to(
            waves[:, chunk * LANES:(chunk + 1) * LANES], (STRIP, LANES)
        ).astype(jnp.float32)
        length = jnp.zeros((STRIP, LANES), jnp.int32)
        for r in range(STRIP):
            place = jnp.where(south, STRIP - 1 - r, r)
            length = jnp.where(backward == place, row_length(r), length)
        length = length.astype(jnp.float32)
        factor = jnp.where(2.0 * m16 < length, 1.0 / length, 0.0)
        for k in range(6):
            total = sums[k, pl.ds(0, STRIP, stride=8), :]
            for s in range(1, 8):
                total = total + sums[k, pl.ds(s, STRIP, stride=8), :]
            at = pl.ds(pl.multiple_of(k * rows + block, STRIP), STRIP)
            gathered[chunk, at, :] = total * factor

    @pl.when(step == 0)
    def _():
        tail = gathered.shape[1] - 6 * rows
        if tail:
            for chunk in range(chunks):
                gathered[chunk, 6 * rows:, :] = jnp.zeros((tail, LANES), jnp.float32)

    @pl.when(step == steps - 1)
    def _():
        for chunk in range(chunks):
            for b in range(gathered.shape[1] // LANES):
                turned = gathered[chunk, b * LANES:(b + 1) * LANES, :].T.astype(out.dtype)
                slots = out.shape[1]
                owners = LANES // slots
                out[chunk * owners:(chunk + 1) * owners, :, b * LANES:(b + 1) * LANES] = (
                    turned.reshape(owners, slots, LANES)
                )


def legendre(rows, waves_total, orders, got, table, out, first_kept, second_kept):
    levels = lax.axis_size("lev")
    bands = lax.axis_size("wide")
    slots = got.shape[1]
    device = lax.axis_index("wide") * levels + lax.axis_index("lev")
    half = bands // 2
    tall = levels * slots

    def band_fields(w):
        parts = [got[w * levels + l].astype(jnp.float32) for l in range(levels)]
        under = jnp.zeros((slots, 2 * rows), jnp.float32)
        energy = []
        for l in reversed(range(levels)):
            energy.append(parts[l][:, :2 * rows] + under)
            under = under + parts[l][:, 2 * rows:4 * rows]
        energy = jnp.concatenate(energy[::-1], axis=0)
        flux = jnp.concatenate([p[:, 4 * rows:6 * rows] for p in parts], axis=0)
        both = jnp.concatenate([energy, flux], axis=0)
        return jnp.concatenate([both[:, :rows], both[:, rows:]], axis=0)

    lefts = []
    for w in range(half):
        north = band_fields(w)
        south = band_fields(bands - 1 - w)
        lefts.append(jnp.concatenate([north + south, north - south], axis=0).astype(jnp.bfloat16))
    deep = 4 * tall
    for q in range(slots // 2):
        first = orders[device * slots + 2 * q]
        split = waves_total - first
        for chunk in range(table.shape[2] // LANES):
            cols = slice(chunk * LANES, (chunk + 1) * LANES)
            total = jnp.zeros((2 * deep, LANES), jnp.float32)
            for w in range(half):
                total = total + jnp.dot(
                    lefts[w],
                    table[q, w * rows:(w + 1) * rows, cols],
                    preferred_element_type=jnp.float32,
                )
            even = total[:deep]
            odd = total[deep:]
            column = lax.broadcasted_iota(jnp.int32, (deep, LANES), 1) + chunk * LANES
            shifted = column + split
            first_kept[...] = jnp.where((column & 1) == 0, even, odd)
            second_kept[...] = jnp.where((shifted & 1) == 0, even, odd)
            one = first_kept[pl.ds(2 * q, 4 * levels, stride=slots), :]
            two = second_kept[pl.ds(2 * q + 1, 4 * levels, stride=slots), :]
            column = lax.broadcasted_iota(jnp.int32, one.shape, 1) + chunk * LANES
            result = jnp.where(column < split, one, two)
            result = jnp.where(column <= waves_total, result, 0.0)
            out[q, :, cols] = result.astype(out.dtype)


def local(u, v, temp, oro, depths, lens, orders, table):
    lev_count = lax.axis_size("lev")
    wide_count = lax.axis_size("wide")
    lev = lax.axis_index("lev")
    wide = lax.axis_index("wide")
    rows = temp.shape[1]
    samples = temp.shape[2]
    waves_total = orders.shape[0]
    high = samples // LANES
    high_pad = -(-high // 8) * 8
    steps = rows // STRIP
    devices = lev_count * wide_count
    slots = waves_total // devices
    packed = -(-6 * rows // LANES) * LANES
    held = lens.reshape(1, 1, lens.shape[0])
    band = exchange(held, ("lev",), lev_count, 1)
    smem = pl.BlockSpec(memory_space=pltpu.SMEM)
    field = pl.BlockSpec((STRIP, samples), lambda i: (i, 0))
    field3 = pl.BlockSpec((None, STRIP, samples), lambda i: (0, i, 0))
    coefs = pl.pallas_call(
        functools.partial(transform, high, high_pad),
        grid=(steps,),
        out_shape=jax.ShapeDtypeStruct((devices, slots, packed), jnp.bfloat16),
        in_specs=[
            smem,
            smem,
            pl.BlockSpec((1, waves_total), lambda i: (0, 0)),
            field3,
            field3,
            field3,
            field,
        ],
        out_specs=pl.BlockSpec((devices, slots, packed), lambda i: (0, 0, 0)),
        scratch_shapes=[
            pltpu.VMEM((3, high_pad * STRIP, LANES), jnp.float32),
            pltpu.VMEM((6, STRIP * 8, LANES), jnp.float32),
            pltpu.VMEM((waves_total // LANES, packed, LANES), jnp.float32),
        ],
        compiler_params=pltpu.CompilerParams(vmem_limit_bytes=60 * 2**20),
    )(
        band,
        depths,
        orders[None],
        u,
        v,
        temp,
        oro,
    )
    got = exchange(coefs, ("wide", "lev"), devices, 0)
    pairs = slots // 2
    width = table.shape[2]
    vmem = pl.BlockSpec(memory_space=pltpu.VMEM)
    kept = pltpu.VMEM((4 * lev_count * slots, LANES), jnp.float32)
    result = pl.pallas_call(
        functools.partial(legendre, rows, waves_total),
        out_shape=jax.ShapeDtypeStruct((pairs, 4 * lev_count, width), jnp.bfloat16),
        in_specs=[smem, vmem, vmem],
        out_specs=vmem,
        scratch_shapes=[kept, kept],
        compiler_params=pltpu.CompilerParams(vmem_limit_bytes=60 * 2**20),
    )(orders, got, table)
    return result.reshape(pairs, 2, 2, lev_count, width).transpose(0, 1, 3, 2, 4)


def solution(mesh):
    in_specs = (
        P("lev", "wide", None),
        P("lev", "wide", None),
        P("lev", "wide", None),
        P("wide", None),
        P(),
        P(("wide", "lev")),
        P(),
        P(("wide", "lev"), None, None),
    )
    out_specs = P(("wide", "lev"), None, None, None, None)
    return jax.shard_map(local, mesh=mesh, in_specs=in_specs, out_specs=out_specs, check_vma=False)
```

```python
import functools

import jax
import jax.numpy as jnp
from jax import lax
from jax.experimental import pallas as pl
from jax.experimental.pallas import tpu as pltpu
from jax.sharding import PartitionSpec as P

STRIP = 16
LANES = 128
COS = (0.9999992251396179, -19.738981246948242, 64.92865753173828, -85.27162170410156, 58.79049301147461, -21.07110595703125)
SIN = (6.283185005187988, -41.341590881347656, 81.59994506835938, -76.61447143554688, 41.3428840637207, -12.471243858337402)


def horner(coefs, z):
    value = jnp.full_like(z, coefs[-1])
    for c in coefs[-2::-1]:
        value = value * z + c
    return value


def unit(n, length, inverse):
    turns = jnp.round(n * inverse)
    t = (n - turns * length) * inverse
    z = t * t
    return horner(COS, z), t * horner(SIN, z)


def times(a, b):
    return a[0] * b[0] - a[1] * b[1], a[0] * b[1] + a[1] * b[0]


MESH = pl.DeviceIdType.MESH


def swap(axes, x, out, landed, send_sem, recv_sem):
    sizes = [lax.axis_size(a) for a in axes]
    count = 1
    me = 0
    for a, size in zip(axes, sizes):
        count = count * size
        me = me * size + lax.axis_index(a)
    shared = x.shape[0] != count

    def device(turn):
        peer = lax.rem(me + turn, count)
        if len(axes) == 1:
            return peer, {axes[0]: peer}
        return peer, {axes[0]: lax.div(peer, sizes[1]), axes[1]: lax.rem(peer, sizes[1])}

    barrier = pltpu.get_barrier_semaphore()

    def greet(turn, carry):
        pl.semaphore_signal(barrier, inc=1, device_id=device(turn)[1], device_id_type=MESH)
        return carry

    lax.fori_loop(1, count, greet, 0)
    pl.semaphore_wait(barrier, count - 1)

    def copy(turn):
        peer, where = device(turn)
        return pltpu.make_async_remote_copy(
            src_ref=x.at[0 if shared else peer],
            dst_ref=landed.at[me],
            send_sem=send_sem.at[turn],
            recv_sem=recv_sem.at[turn],
            device_id=where,
            device_id_type=MESH,
        )

    def begin(step, carry):
        copy(1 + lax.rem(step + count // 2 - 1, count - 1)).start()
        return carry

    def finish(turn, carry):
        copy(turn).wait()
        return carry

    lax.fori_loop(0, count - 1, begin, 0)
    landed[me] = x[0 if shared else me]
    lax.fori_loop(1, count, finish, 0)
    out[...] = landed[...]


def exchange(x, axes, count, number):
    shape = (count,) + x.shape[1:]
    vmem = pl.BlockSpec(memory_space=pltpu.VMEM)
    return pl.pallas_call(
        functools.partial(swap, axes),
        out_shape=jax.ShapeDtypeStruct(shape, x.dtype),
        in_specs=[vmem],
        out_specs=vmem,
        scratch_shapes=[
            pltpu.VMEM(shape, x.dtype),
            pltpu.SemaphoreType.DMA((count,)),
            pltpu.SemaphoreType.DMA((count,)),
        ],
        compiler_params=pltpu.CompilerParams(
            collective_id=number, has_side_effects=True, vmem_limit_bytes=24 * 2**20
        ),
    )(x)


def transform(high, high_pad, lens, depths, waves, u, v, temp, oro, out, spread, sums, gathered):
    step = pl.program_id(0)
    steps = pl.num_programs(0)
    rows = steps * STRIP
    south = lax.axis_index("wide") * 2 >= lax.axis_size("wide")
    level = lax.axis_index("lev")
    depth = depths[level]
    ground = jnp.where(level == lax.axis_size("lev") - 1, 1.0, 0.0)
    share = rows // lens.shape[0]

    def row_length(r):
        row = step * STRIP + r
        return lens[lax.div(row, share), 0, lax.rem(row, share)]

    backward = lax.broadcasted_iota(jnp.int32, (STRIP, LANES), 0)
    limit = jnp.zeros((STRIP, LANES), jnp.int32)
    for r in range(STRIP):
        limit = jnp.where(backward == r, row_length(r), limit)
    lane = lax.broadcasted_iota(jnp.int32, (STRIP, LANES), 1)
    for h in range(high_pad):
        at = pl.ds(h * STRIP, STRIP)
        if h >= high:
            for c in range(3):
                spread[c, at, :] = jnp.zeros((STRIP, LANES), jnp.float32)
            continue
        cols = pl.ds(h * LANES, LANES)
        east = u[:, cols].astype(jnp.float32)
        north = v[:, cols].astype(jnp.float32)
        heat = temp[:, cols].astype(jnp.float32)
        weighted = heat * depth + oro[:, cols].astype(jnp.float32) * ground
        energy = 0.5 * (east * east + north * north) + weighted
        inside = lane + h * LANES < limit
        spread[0, at, :] = jnp.where(inside, energy, 0.0)
        spread[1, at, :] = jnp.where(inside, weighted, 0.0)
        spread[2, at, :] = jnp.where(inside, north * heat, 0.0)

    sub = lax.broadcasted_iota(jnp.int32, (8, LANES), 0).astype(jnp.float32)
    chunks = waves.shape[1] // LANES
    for chunk in range(chunks):
        m = jnp.broadcast_to(waves[:, chunk * LANES:(chunk + 1) * LANES], (8, LANES)).astype(jnp.float32)

        def one_row(r, carry):
            length = jnp.broadcast_to(row_length(r).astype(jnp.float32), (8, LANES))
            inverse = 1.0 / length
            data = jnp.concatenate(
                [spread[c, pl.ds(r, high_pad, stride=STRIP), :] for c in range(3)], axis=0
            ).astype(jnp.bfloat16)
            tiles = [unit(m * sub, length, inverse)]
            turn = unit(m * 8.0, length, inverse)
            while len(tiles) < LANES // 8:
                tiles = tiles + [times(tile, turn) for tile in tiles]
                turn = times(turn, turn)
            table = jnp.concatenate(
                [
                    jnp.concatenate([tile[0] for tile in tiles], axis=0),
                    jnp.concatenate([tile[1] for tile in tiles], axis=0),
                ],
                axis=1,
            ).astype(jnp.bfloat16)
            part = jnp.dot(data, table, preferred_element_type=jnp.float32)
            outer = [unit(m * (sub * float(LANES)), length, inverse)]
            stride = unit(m * float(8 * LANES), length, inverse)
            while len(outer) < high_pad // 8:
                outer.append(times(outer[-1], stride))
            place = jnp.where(south, STRIP - 1 - r, r)
            for c in range(3):
                real = jnp.zeros((8, LANES), jnp.float32)
                imag = jnp.zeros((8, LANES), jnp.float32)
                for g in range(high_pad // 8):
                    base = c * high_pad + g * 8
                    pc = part[base:base + 8, :LANES]
                    ps = part[base:base + 8, LANES:]
                    oc, os = outer[g]
                    real = real + (pc * oc - ps * os)
                    imag = imag - (pc * os + ps * oc)
                at = pl.ds(pl.multiple_of(place * 8, 8), 8)
                sums[2 * c, at, :] = real
                sums[2 * c + 1, at, :] = imag
            return carry

        lax.fori_loop(0, STRIP, one_row, 0, unroll=8)

        block = jnp.where(south, steps - 1 - step, step) * STRIP
        m16 = jnp.broadcast_to(
            waves[:, chunk * LANES:(chunk + 1) * LANES], (STRIP, LANES)
        ).astype(jnp.float32)
        length = jnp.zeros((STRIP, LANES), jnp.int32)
        for r in range(STRIP):
            place = jnp.where(south, STRIP - 1 - r, r)
            length = jnp.where(backward == place, row_length(r), length)
        length = length.astype(jnp.float32)
        factor = jnp.where(2.0 * m16 < length, 1.0 / length, 0.0)
        for k in range(6):
            total = sums[k, pl.ds(0, STRIP, stride=8), :]
            for s in range(1, 8):
                total = total + sums[k, pl.ds(s, STRIP, stride=8), :]
            at = pl.ds(pl.multiple_of(k * rows + block, STRIP), STRIP)
            gathered[chunk, at, :] = total * factor

    @pl.when(step == 0)
    def _():
        tail = gathered.shape[1] - 6 * rows
        if tail:
            for chunk in range(chunks):
                gathered[chunk, 6 * rows:, :] = jnp.zeros((tail, LANES), jnp.float32)

    @pl.when(step == steps - 1)
    def _():
        for chunk in range(chunks):
            for b in range(gathered.shape[1] // LANES):
                turned = gathered[chunk, b * LANES:(b + 1) * LANES, :].T.astype(out.dtype)
                slots = out.shape[1]
                owners = LANES // slots
                out[chunk * owners:(chunk + 1) * owners, :, b * LANES:(b + 1) * LANES] = (
                    turned.reshape(owners, slots, LANES)
                )


def legendre(rows, waves_total, orders, got, table, out, first_kept, second_kept):
    levels = lax.axis_size("lev")
    bands = lax.axis_size("wide")
    slots = got.shape[1]
    device = lax.axis_index("wide") * levels + lax.axis_index("lev")
    half = bands // 2
    tall = levels * slots

    def band_fields(w):
        parts = [got[w * levels + l].astype(jnp.float32) for l in range(levels)]
        under = jnp.zeros((slots, 2 * rows), jnp.float32)
        energy = []
        for l in reversed(range(levels)):
            energy.append(parts[l][:, :2 * rows] + under)
            under = under + parts[l][:, 2 * rows:4 * rows]
        energy = jnp.concatenate(energy[::-1], axis=0)
        flux = jnp.concatenate([p[:, 4 * rows:6 * rows] for p in parts], axis=0)
        both = jnp.concatenate([energy, flux], axis=0)
        return jnp.concatenate([both[:, :rows], both[:, rows:]], axis=0)

    lefts = []
    for w in range(half):
        north = band_fields(w)
        south = band_fields(bands - 1 - w)
        lefts.append(jnp.concatenate([north + south, north - south], axis=0).astype(jnp.bfloat16))
    deep = 4 * tall
    for q in range(slots // 2):
        first = orders[device * slots + 2 * q]
        split = waves_total - first
        for chunk in range(table.shape[2] // LANES):
            cols = slice(chunk * LANES, (chunk + 1) * LANES)
            total = jnp.zeros((2 * deep, LANES), jnp.float32)
            for w in range(half):
                total = total + jnp.dot(
                    lefts[w],
                    table[q, w * rows:(w + 1) * rows, cols],
                    preferred_element_type=jnp.float32,
                )
            even = total[:deep]
            odd = total[deep:]
            column = lax.broadcasted_iota(jnp.int32, (deep, LANES), 1) + chunk * LANES
            shifted = column + split
            first_kept[...] = jnp.where((column & 1) == 0, even, odd)
            second_kept[...] = jnp.where((shifted & 1) == 0, even, odd)
            one = first_kept[pl.ds(2 * q, 4 * levels, stride=slots), :]
            two = second_kept[pl.ds(2 * q + 1, 4 * levels, stride=slots), :]
            column = lax.broadcasted_iota(jnp.int32, one.shape, 1) + chunk * LANES
            result = jnp.where(column < split, one, two)
            result = jnp.where(column <= waves_total, result, 0.0)
            out[q, :, cols] = result.astype(out.dtype)


def local(u, v, temp, oro, depths, lens, orders, table):
    lev_count = lax.axis_size("lev")
    wide_count = lax.axis_size("wide")
    lev = lax.axis_index("lev")
    wide = lax.axis_index("wide")
    rows = temp.shape[1]
    samples = temp.shape[2]
    waves_total = orders.shape[0]
    high = samples // LANES
    high_pad = -(-high // 8) * 8
    steps = rows // STRIP
    devices = lev_count * wide_count
    slots = waves_total // devices
    packed = -(-6 * rows // LANES) * LANES
    held = lens.reshape(1, 1, lens.shape[0])
    band = exchange(held, ("lev",), lev_count, 1)
    smem = pl.BlockSpec(memory_space=pltpu.SMEM)
    field = pl.BlockSpec((STRIP, samples), lambda i: (i, 0))
    field3 = pl.BlockSpec((None, STRIP, samples), lambda i: (0, i, 0))
    coefs = pl.pallas_call(
        functools.partial(transform, high, high_pad),
        grid=(steps,),
        out_shape=jax.ShapeDtypeStruct((devices, slots, packed), jnp.bfloat16),
        in_specs=[
            smem,
            smem,
            pl.BlockSpec((1, waves_total), lambda i: (0, 0)),
            field3,
            field3,
            field3,
            field,
        ],
        out_specs=pl.BlockSpec((devices, slots, packed), lambda i: (0, 0, 0)),
        scratch_shapes=[
            pltpu.VMEM((3, high_pad * STRIP, LANES), jnp.float32),
            pltpu.VMEM((6, STRIP * 8, LANES), jnp.float32),
            pltpu.VMEM((waves_total // LANES, packed, LANES), jnp.float32),
        ],
        compiler_params=pltpu.CompilerParams(vmem_limit_bytes=60 * 2**20),
    )(
        band,
        depths,
        orders[None],
        u,
        v,
        temp,
        oro,
    )
    got = exchange(coefs, ("wide", "lev"), devices, 0)
    pairs = slots // 2
    width = table.shape[2]
    vmem = pl.BlockSpec(memory_space=pltpu.VMEM)
    kept = pltpu.VMEM((4 * lev_count * slots, LANES), jnp.float32)
    result = pl.pallas_call(
        functools.partial(legendre, rows, waves_total),
        out_shape=jax.ShapeDtypeStruct((pairs, 4 * lev_count, width), jnp.bfloat16),
        in_specs=[smem, vmem, vmem],
        out_specs=vmem,
        scratch_shapes=[kept, kept],
        compiler_params=pltpu.CompilerParams(vmem_limit_bytes=40 * 2**20),
    )(orders, got, table)
    return result.reshape(pairs, 2, 2, lev_count, width).transpose(0, 1, 3, 2, 4)


def solution(mesh):
    in_specs = (
        P("lev", "wide", None),
        P("lev", "wide", None),
        P("lev", "wide", None),
        P("wide", None),
        P(),
        P(("wide", "lev")),
        P(),
        P(("wide", "lev"), None, None),
    )
    out_specs = P(("wide", "lev"), None, None, None, None)
    return jax.shard_map(local, mesh=mesh, in_specs=in_specs, out_specs=out_specs, check_vma=False)
```
